128 devices in a mesh: gx: 8 (over z_lo, y), gy: 16 (over x, z_hi, core).
Axes of the slice: x: 4, y: 4, z: 4 (z_hi: 2, z_lo: 2; z = z_hi * 2 + z_lo), core: 2. Of those that a mesh axis runs over, the one named last changes fastest.
Arguments:
- levels: int32 [8, 128, 16384], P(None, 'gx', 'gy'), may hold values from 0 to 7
- probe_bits: int32 [8, 8, 128, 16384], P(None, None, 'gx', 'gy'), may hold values from 0 to 1
Outputs:
- green: float32 [2, 8192, 64], P(None, ('gx', 'gy'))
- last_vector: float32 [8, 8, 128, 16384], P(None, None, 'gx', 'gy')
The draws below stay inside these ranges and needn't reach their ends.
All inputs are finite; a program needn't handle non-finite values.
Results may differ from the reference program's by a relative error of at most 0.00011.
Values sent between devices are 32-bit elements; how exact they have to be, the bound alone decides.
A program may use at most 128 MiB of HBM per device.

```python
import math
import jax
import jax.numpy as jnp
from jax import lax

PROBES = 8
PL = 8
STEPS = 4
LEVELS = 8
NE = 8192
NMOM = 8
NX = 128
NY = 16384
SITES = 16777216


def draw_levels(key, part):
    plane_key, span_key, fine_key = jax.random.split(jax.random.fold_in(key, 11), 3)
    base = jax.random.randint(plane_key, (PL, 1, 1), 0, LEVELS)
    span = jax.random.randint(span_key, (PL, 1, 1), 2, LEVELS + 1)
    fine = jax.random.randint(fine_key, (PL, NX, NY), 0, 1 << 20)
    return ((base + fine % span) % LEVELS).astype(jnp.int32)


def draw_probe_bits(key, part):
    coarse_key, rate_key, flip_key = jax.random.split(jax.random.fold_in(key, 23), 3)
    coarse = jax.random.randint(coarse_key, (PL, NX // 2, NY // 4), 0, 2)
    common = jnp.repeat(jnp.repeat(coarse, 2, axis=1), 4, axis=2)
    rates = jax.random.randint(rate_key, (PROBES, 1, 1, 1), 1, 8)
    flips = (jax.random.randint(flip_key, (PROBES, PL, NX, NY), 0, 16) < rates).astype(jnp.int32)
    return ((common[None] + flips) % 2).astype(jnp.int32)


def block_levels(rng, shape, cuts, least, high):
    level, own = 1.0, jax.random.fold_in(rng, 6)
    for dim, parts in cuts:
        draws = jnp.exp(jax.random.uniform(jax.random.fold_in(own, dim), (parts,), jnp.float32, least / len(cuts), high / len(cuts)))
        level = level * jnp.repeat(draws, shape[dim] // parts).reshape([-1 if axis == dim else 1 for axis in range(len(shape))])
    return level


def setup_inputs(seed: int = 0) -> dict:
    streams_of = jax.random.split(jax.random.key(seed), 3)
    return {
        "levels": draw_levels(jax.random.fold_in(streams_of[2], 71), 0),
        "probe_bits": draw_probe_bits(jax.random.fold_in(streams_of[2], 71), 0),
    }


disorder_width = 4.0
field_strength = 3.0
spectral_scale = 10.0
energy_edge = 0.9


def jackson_weights(count):
    total = count + 1.0
    values = []
    for order in range(count):
        damping = ((count - order + 1.0) * math.cos(math.pi * order / total) + math.sin(math.pi * order / total) / math.tan(math.pi / total)) / total
        values.append(damping if order == 0 else 2.0 * damping)
    return jnp.asarray(values, dtype=jnp.float32)


def energy_tables(energy_index, count, total_energies):
    phase = math.pi * (energy_index.astype(jnp.float32) + 0.5) / total_energies
    theta = jnp.arccos(energy_edge * jnp.cos(phase))
    orders = jnp.arange(count).astype(jnp.float32)
    weights = jackson_weights(count)
    angles = theta[:, None] * orders[None, :]
    denominator = jnp.sin(theta)[:, None]
    real_part = -weights[None, :] * jnp.sin(angles) / denominator
    imag_part = -weights[None, :] * jnp.cos(angles) / denominator
    return real_part, imag_part


def hopping(field, onsite):
    beside = jnp.roll(field, -1, 2) + jnp.roll(field, 1, 2)
    beside = beside + jnp.roll(field, -1, 3) + jnp.roll(field, 1, 3)
    zeros_plane = jnp.zeros_like(field[:, :1])
    beside = beside + jnp.concatenate([field[:, 1:], zeros_plane], 1)
    beside = beside + jnp.concatenate([zeros_plane, field[:, :-1]], 1)
    return (onsite[None] * field - beside) / spectral_scale


def inner_matrix(first, second):
    left = first.reshape(first.shape[0], -1)
    right = second.reshape(second.shape[0], -1)
    return jnp.dot(left, right.T, precision=lax.Precision.HIGHEST, preferred_element_type=jnp.float32)


def moments_from(grams, sites):
    first = grams[0] / sites
    second = grams[1] / sites
    result = [first, second]
    for order in range(1, grams.shape[0] // 2):
        result.append(2.0 * grams[2 * order] / sites - first)
        result.append(2.0 * grams[2 * order + 1] / sites - second)
    stacked = jnp.stack(result)
    return stacked.reshape(stacked.shape[0], -1)


def reference(levels, probe_bits):
    row_index = jnp.arange(NX).astype(jnp.float32)
    onsite = disorder_width * (levels.astype(jnp.float32) / (LEVELS - 1) - 0.5) + field_strength * ((row_index + 0.5) / NX - 0.5)[None, :, None]
    vectors = [(2 * probe_bits - 1).astype(jnp.float32)]
    for step in range(STEPS):
        hopped = hopping(vectors[-1], onsite)
        if step == 0:
            vectors.append(hopped)
        else:
            vectors.append(2.0 * hopped - vectors[-2])
    grams = []
    for step in range(STEPS):
        grams.append(inner_matrix(vectors[step], vectors[step]))
        grams.append(inner_matrix(vectors[step], vectors[step + 1]))
    moments = moments_from(jnp.stack(grams), SITES)
    real_part, imag_part = energy_tables(jnp.arange(NE).astype(jnp.int32), NMOM, NE)
    green_real = jnp.dot(real_part, moments, precision=lax.Precision.HIGHEST, preferred_element_type=jnp.float32)
    green_imag = jnp.dot(imag_part, moments, precision=lax.Precision.HIGHEST, preferred_element_type=jnp.float32)
    return jnp.stack([green_real, green_imag]), vectors[-1]
```

```python
import functools
import math

import jax
import jax.numpy as jnp
import numpy as np
from jax import lax
from jax.experimental import pallas as pl
from jax.experimental.pallas import tpu as pltpu
from jax.sharding import PartitionSpec as P

PROBES = 8
PL = 8
STEPS = 4
LEVELS = 8
NE = 8192
NMOM = 8
NX = 128
NY = 16384
SITES = 16777216
GXN = 8
GYN = 16
ROWS = NX // GXN
COLS = NY // GYN
TILES = COLS // 128
EB = NE // (GXN * GYN)
SPAN = PL + 1
GROUP = 4

disorder_width = 4.0
field_strength = 3.0
spectral_scale = 10.0
energy_edge = 0.9

MESH = pl.DeviceIdType.MESH
F32 = jnp.float32
BF16 = jnp.bfloat16


def energy_tables():
    theta = np.arccos(energy_edge * np.cos(math.pi * (np.arange(NE) + 0.5) / NE))
    total = NMOM + 1.0
    rows = []
    for m in range(NMOM):
        damp = (
            (NMOM - m + 1.0) * math.cos(math.pi * m / total)
            + math.sin(math.pi * m / total) / math.tan(math.pi / total)
        ) / total
        weight = damp if m == 0 else 2.0 * damp
        rows.append(
            np.stack(
                [
                    -weight * np.sin(m * theta) / np.sin(theta),
                    -weight * np.cos(m * theta) / np.sin(theta),
                ]
            )
        )
    table = np.stack(rows).reshape(NMOM, 2, GXN * GYN, EB)
    return np.ascontiguousarray(table.transpose(2, 0, 1, 3).reshape(GXN * GYN, NMOM, 2 * EB)).astype(np.float32)


def lanes():
    return lax.broadcasted_iota(jnp.int32, (8, 128), 1)


def split(pair):
    high = pair.astype(BF16)
    return high, (pair - high.astype(F32)).astype(BF16)


def main_kernel(
    levels, bits, last, moments_out,
    field, raw, halves, onsite, lev, edge_out, edge_in, grams, flat, first, second,
    row_send, row_recv, col_send, col_recv, load_sem, lev_sem, sum_send, sum_recv,
):
    gx, gy = lax.axis_index("gx"), lax.axis_index("gy")
    up, down = (lax.rem(gx + GXN - 1, GXN), gy), (lax.rem(gx + 1, GXN), gy)
    left, right = (gx, lax.rem(gy + GYN - 1, GYN)), (gx, lax.rem(gy + 1, GYN))

    def row_copy(n, p, side):
        target = (up, down)[side]
        here, there = ((1, ROWS + 1), (ROWS, 0))[side]
        if n == 0:
            src, dst = bits.at[:, p, here - 1, :], raw.at[p, there]
        else:
            src, dst = field.at[n * SPAN + 1 + p, here], field.at[n * SPAN + 1 + p, there]
        return pltpu.make_async_remote_copy(
            src, dst, row_send.at[n, side, p], row_recv.at[n, side, p],
            device_id=target, device_id_type=MESH,
        )

    def col_copy(n, p, side):
        return pltpu.make_async_remote_copy(
            edge_out.at[n, side, p], edge_in.at[n, side, p],
            col_send.at[n, side, p], col_recv.at[n, side, p],
            device_id=(left, right)[side], device_id_type=MESH,
        )

    def load(p, i):
        return pltpu.make_async_copy(bits.at[i, p], raw.at[p, pl.ds(1, ROWS), i, :], load_sem.at[p, i])

    barrier = pltpu.get_barrier_semaphore()
    for d in range(1, GXN):
        pl.semaphore_signal(barrier, inc=1, device_id=(lax.rem(gx + d, GXN), gy), device_id_type=MESH)
    for d in range(1, GYN):
        pl.semaphore_signal(barrier, inc=1, device_id=(gx, lax.rem(gy + d, GYN)), device_id_type=MESH)

    lev_copy = pltpu.make_async_copy(levels, lev, lev_sem)
    lev_copy.start()

    @pl.loop(0, PL)
    def _(p):
        for i in range(PROBES):
            load(p, i).start()

    pl.semaphore_wait(barrier, GXN + GYN - 2)

    @pl.loop(0, PL)
    def _(p):
        for side in range(2):
            row_copy(0, p, side).start()

    @pl.loop(0, STEPS + 1)
    def _(n):
        field[n * SPAN] = jnp.zeros((ROWS + 2, PROBES, COLS), F32)

    grams[...] = jnp.zeros_like(grams)
    flat[...] = jnp.zeros_like(flat)
    lev_copy.wait()

    @pl.loop(0, PL)
    def _(p):
        for i in range(PROBES):
            load(p, i).wait()

        def rows(g, edges):
            left_edge, right_edge = edges
            lane = lanes()
            for k in range(0, GROUP, 2):
                x = g * GROUP + k
                at = pl.multiple_of(x * PROBES, 16)
                for c in range(TILES):
                    cut = pl.ds(c * 128, 128)
                    pair = []
                    for q in (0, 1):
                        value = (2 * raw[p, x + q + 1, :, cut] - 1).astype(F32)
                        field[p + 1, x + q + 1, :, cut] = value
                        pair.append(value)
                        if c == 0:
                            left_edge = jnp.where(lane == x + q, pltpu.roll(value, x + q, 1), left_edge)
                        if c == TILES - 1:
                            right_edge = jnp.where(lane == x + q, pltpu.roll(value, x + q + 1, 1), right_edge)
                    halves[0, p, pl.ds(at, 16), cut] = jnp.concatenate(pair, 0).astype(BF16)
            return left_edge, right_edge

        zero = jnp.zeros((8, 128), F32)
        left_edge, right_edge = lax.fori_loop(0, ROWS // GROUP, rows, (zero, zero))
        edge_out[0, 0, p] = left_edge
        edge_out[0, 1, p] = right_edge
        for side in range(2):
            col_copy(0, p, side).start()
        for x in range(ROWS):
            row = (gx * ROWS + x).astype(F32)
            slope = field_strength * ((row + 0.5) / NX - 0.5)
            value = disorder_width * (lev[p, pl.ds(x, 1), :].astype(F32) / (LEVELS - 1) - 0.5) + slope
            onsite[p, x] = jnp.broadcast_to(value, (PROBES, COLS))

    def step(n, p):
        base = n * SPAN + 1 + p
        for side in range(2):
            row_copy(n, p, side).wait_recv()
            col_copy(n, p, side).wait_recv()
        if n == 0:
            for x in (0, ROWS + 1):
                field[base, x] = (2 * raw[p, x] - 1).astype(F32)
        from_right, from_left = edge_in[n, 0, p], edge_in[n, 1, p]

        def rows(g, edges):
            left_edge, right_edge = edges
            lane = lanes()
            is_first, is_last = lane == 0, lane == 127
            x0 = g * GROUP

            def column(c):
                return [field[base, x0 + k, :, pl.ds(c * 128, 128)] for k in range(GROUP + 2)]

            own = range(1, GROUP + 1)
            before = [pltpu.roll(from_left, lax.rem(128 - (x0 + k - 1), 128), 1) for k in own]
            beyond = [pltpu.roll(from_right, 127 - (x0 + k - 1), 1) for k in own]
            now = column(0)
            forth = [pltpu.roll(now[k], 1, 1) for k in own]
            back = [pltpu.roll(now[k], 127, 1) for k in own]
            for c in range(TILES):
                cut = pl.ds(c * 128, 128)
                if c + 1 < TILES:
                    later = column(c + 1)
                    later_forth = [pltpu.roll(later[k], 1, 1) for k in own]
                    later_back = [pltpu.roll(later[k], 127, 1) for k in own]
                else:
                    later, later_forth, later_back = None, None, beyond
                made = []
                for k in own:
                    x = x0 + k - 1
                    beside = now[k + 1] + now[k - 1]
                    beside = beside + jnp.where(is_last, later_back[k - 1], back[k - 1])
                    beside = beside + jnp.where(is_first, before[k - 1], forth[k - 1])
                    beside = beside + field[base + 1, x + 1, :, cut]
                    beside = beside + field[base - 1, x + 1, :, cut]
                    hopped = onsite[p, x, :, cut] * now[k] - beside
                    if n == 0:
                        value = hopped * (1.0 / spectral_scale)
                    else:
                        value = hopped * (2.0 / spectral_scale) - field[base - SPAN, x + 1, :, cut]
                    if n + 1 < STEPS:
                        field[base + SPAN, x + 1, :, cut] = value
                        if c == 0:
                            left_edge = jnp.where(lane == x, pltpu.roll(value, x, 1), left_edge)
                        if c == TILES - 1:
                            right_edge = jnp.where(lane == x, pltpu.roll(value, x + 1, 1), right_edge)
                    else:
                        last[p, x, :, cut] = value
                    made.append(value)
                for k in range(0, GROUP, 2):
                    high, low = split(jnp.concatenate(made[k : k + 2], 0))
                    at = pl.multiple_of((x0 + k) * PROBES, 16)
                    halves[(n + 1) % 2, p, pl.ds(at, 16), cut] = high
                    halves[(n + 1) % 2, p, pl.ds(ROWS * PROBES + at, 16), cut] = low
                now, before, forth, back = later, forth, later_forth, later_back
            return left_edge, right_edge

        zero = jnp.zeros((8, 128), F32)
        left_edge, right_edge = lax.fori_loop(0, ROWS // GROUP, rows, (zero, zero))
        if n + 1 < STEPS:
            edge_out[n + 1, 0, p] = left_edge
            edge_out[n + 1, 1, p] = right_edge
            for side in range(2):
                row_copy(n + 1, p, side).start()
                col_copy(n + 1, p, side).start()

        lane_group = lanes() // PROBES
        held = ROWS * PROBES if n == 0 else 2 * ROWS * PROBES
        stays = halves[n % 2, p, 0:held]
        for which, other in ((0, stays), (1, halves[(n + 1) % 2, p])):
            product = lax.dot_general(stays, other, (((1,), (1,)), ((), ())), preferred_element_type=F32)
            total = None
            for part in range(0, product.shape[0], ROWS * PROBES):
                for c in range(0, product.shape[1], 128):
                    chosen = product[part : part + PROBES, c : c + 128]
                    for x in range(1, ROWS):
                        block = product[part + x * PROBES : part + (x + 1) * PROBES, c : c + 128]
                        chosen = jnp.where(lane_group == x, block, chosen)
                    total = chosen if total is None else total + chosen
            grams[2 * n + which] += total

    for n in range(STEPS):
        pl.loop(0, PL)(functools.partial(step, n))

    lane, sub = lanes(), lax.broadcasted_iota(jnp.int32, (8, 128), 0)
    keep = sub == lane // PROBES
    packed = jnp.zeros((8, 128), F32)
    for m in range(NMOM):
        total = grams[m]
        for shift in (8, 16, 32, 64):
            total = total + pltpu.roll(total, shift, 1)
        row = jnp.sum(jnp.where(keep, total, 0.0), axis=0, keepdims=True)
        packed = jnp.where(sub == m, jnp.broadcast_to(row, (8, 128)), packed)
    flat[...] = packed

    first[gy] = packed
    copies = []
    for d in range(1, GYN):
        c = pltpu.make_async_remote_copy(
            flat, first.at[gy], sum_send.at[0, d], sum_recv.at[0, d],
            device_id=(gx, lax.rem(gy + d, GYN)), device_id_type=MESH,
        )
        c.start()
        copies.append(c)
    for d in range(1, GYN):
        pltpu.make_async_remote_copy(
            flat, first.at[lax.rem(gy + GYN - d, GYN)], sum_send.at[0, d], sum_recv.at[0, d],
            device_id=(gx, lax.rem(gy + d, GYN)), device_id_type=MESH,
        ).wait_recv()
    total = first[0]
    for d in range(1, GYN):
        total = total + first[d]
    second[gx] = total
    for d in range(1, GXN):
        c = pltpu.make_async_remote_copy(
            second.at[gx], second.at[gx], sum_send.at[1, d], sum_recv.at[1, d],
            device_id=(lax.rem(gx + d, GXN), gy), device_id_type=MESH,
        )
        c.start()
        copies.append(c)
    for d in range(1, GXN):
        source = lax.rem(gx + GXN - d, GXN)
        pltpu.make_async_remote_copy(
            second.at[source], second.at[source], sum_send.at[1, d], sum_recv.at[1, d],
            device_id=(lax.rem(gx + d, GXN), gy), device_id_type=MESH,
        ).wait_recv()
    total = second[0]
    for d in range(1, GXN):
        total = total + second[d]
    moments_out[...] = total

    for c in copies:
        c.wait_send()
    for n in range(STEPS):

        @pl.loop(0, PL)
        def _(p):
            for side in range(2):
                row_copy(n, p, side).wait_send()
                col_copy(n, p, side).wait_send()


def finish_kernel(vector, grams, table, green, out, table_here, out_sem, table_sem):
    device = lax.axis_index("gx") * GYN + lax.axis_index("gy")
    fetch = pltpu.make_async_copy(table.at[device], table_here, table_sem)
    fetch.start()
    copies = []
    for p in range(PL):
        for i in range(PROBES):
            c = pltpu.make_async_copy(vector.at[p, :, i, :], out.at[i, p], out_sem.at[p, i])
            c.start()
            copies.append(c)
    fetch.wait()
    scaled = grams[...] / SITES
    rows = [scaled[0:1], scaled[1:2]]
    for m in range(2, NMOM):
        rows.append(2.0 * scaled[m : m + 1] - rows[m % 2])
    moments = jnp.concatenate(rows + [jnp.zeros((128 - NMOM, 128), F32)], 0)
    weights = jnp.transpose(jnp.concatenate([table_here[...], jnp.zeros((128 - NMOM, 128), F32)], 0))
    result = jnp.dot(weights, moments, precision=lax.Precision.HIGHEST, preferred_element_type=F32)
    green[0] = result[0:EB, 0 : PROBES * PROBES]
    green[1] = result[EB : 2 * EB, 0 : PROBES * PROBES]
    for c in copies:
        c.wait()


def on_device(levels, probe_bits):
    anywhere = pl.BlockSpec(memory_space=pl.ANY)
    vmem = pl.BlockSpec(memory_space=pltpu.VMEM)
    dma = pltpu.SemaphoreType.DMA
    last, grams = pl.pallas_call(
        main_kernel,
        out_shape=(
            pltpu.VMEM((PL, ROWS, PROBES, COLS), F32),
            pltpu.VMEM((8, 128), F32),
        ),
        in_specs=[anywhere, anywhere],
        out_specs=(vmem, vmem),
        scratch_shapes=[
            pltpu.VMEM((STEPS * SPAN + 1, ROWS + 2, PROBES, COLS), F32),
            pltpu.VMEM((PL, ROWS + 2, PROBES, COLS), jnp.int32),
            pltpu.VMEM((2, PL, 2 * ROWS * PROBES, COLS), BF16),
            pltpu.VMEM((PL, ROWS, PROBES, COLS), F32),
            pltpu.VMEM((PL, ROWS, COLS), jnp.int32),
            pltpu.VMEM((STEPS, 2, PL, 8, 128), F32),
            pltpu.VMEM((STEPS, 2, PL, 8, 128), F32),
            pltpu.VMEM((NMOM, 8, 128), F32),
            pltpu.VMEM((8, 128), F32),
            pltpu.VMEM((GYN, 8, 128), F32),
            pltpu.VMEM((GXN, 8, 128), F32),
            dma((STEPS, 2, PL)),
            dma((STEPS, 2, PL)),
            dma((STEPS, 2, PL)),
            dma((STEPS, 2, PL)),
            dma((PL, PROBES)),
            dma,
            dma((2, GYN)),
            dma((2, GYN)),
        ],
        compiler_params=pltpu.CompilerParams(
            collective_id=0, has_side_effects=True, vmem_limit_bytes=52 << 20
        ),
    )(levels, probe_bits)
    green, out = pl.pallas_call(
        finish_kernel,
        out_shape=(
            jax.ShapeDtypeStruct((2, EB, PROBES * PROBES), F32),
            jax.ShapeDtypeStruct((PROBES, PL, ROWS, COLS), F32),
        ),
        in_specs=[vmem, vmem, anywhere],
        out_specs=(vmem, anywhere),
        scratch_shapes=[
            pltpu.VMEM((NMOM, 2 * EB), F32),
            dma((PL, PROBES)),
            dma,
        ],
        compiler_params=pltpu.CompilerParams(vmem_limit_bytes=8 << 20),
    )(last, grams, jnp.asarray(energy_tables()))
    return green, out


def solution(mesh):
    return jax.shard_map(
        on_device,
        mesh=mesh,
        in_specs=(P(None, "gx", "gy"), P(None, None, "gx", "gy")),
        out_specs=(P(None, ("gx", "gy"), None), P(None, None, "gx", "gy")),
        check_vma=False,
    )
```

```python
import functools
import math

import jax
import jax.numpy as jnp
import numpy as np
from jax import lax
from jax.experimental import pallas as pl
from jax.experimental.pallas import tpu as pltpu
from jax.sharding import PartitionSpec as P

PROBES = 8
PL = 8
STEPS = 4
LEVELS = 8
NE = 8192
NMOM = 8
NX = 128
NY = 16384
SITES = 16777216
GXN = 8
GYN = 16
ROWS = NX // GXN
COLS = NY // GYN
TILES = COLS // 128
EB = NE // (GXN * GYN)
DEFER = 3
PART = ROWS * PROBES
HALF = 2 * PART
BLOCK = 256

disorder_width = 4.0
field_strength = 3.0
spectral_scale = 10.0
energy_edge = 0.9

MESH = pl.DeviceIdType.MESH
F32 = jnp.float32
BF16 = jnp.bfloat16


def energy_tables():
    theta = np.arccos(energy_edge * np.cos(math.pi * (np.arange(NE) + 0.5) / NE))
    total = NMOM + 1.0
    rows = []
    for m in range(NMOM):
        damp = (
            (NMOM - m + 1.0) * math.cos(math.pi * m / total)
            + math.sin(math.pi * m / total) / math.tan(math.pi / total)
        ) / total
        weight = damp if m == 0 else 2.0 * damp
        rows.append(
            np.stack(
                [
                    -weight * np.sin(m * theta) / np.sin(theta),
                    -weight * np.cos(m * theta) / np.sin(theta),
                ]
            )
        )
    table = np.stack(rows).reshape(NMOM, 2, GXN * GYN, EB)
    return np.ascontiguousarray(table.transpose(2, 0, 1, 3).reshape(GXN * GYN, NMOM, 2 * EB)).astype(np.float32)


def lanes():
    return lax.broadcasted_iota(jnp.int32, (8, 128), 1)


def split(pair):
    high = pair.astype(BF16)
    return high, (pair - high.astype(F32)).astype(BF16)


def main_kernel(
    levels, bits, last, moments_out,
    field0, field1, field2, field3, raw, halves, onsite, lev, mix, unmix,
    edge_out, edge_in, grams, flat, first, second,
    row_send, row_recv, col_send, col_recv, load_sem, lev_sem, sum_send, sum_recv,
):
    fields = (field0, field1, field2, field3)
    gx, gy = lax.axis_index("gx"), lax.axis_index("gy")
    up, down = (lax.rem(gx + GXN - 1, GXN), gy), (lax.rem(gx + 1, GXN), gy)
    left, right = (gx, lax.rem(gy + GYN - 1, GYN)), (gx, lax.rem(gy + 1, GYN))

    def row_copy(n, p, side):
        here, there = ((1, ROWS + 1), (ROWS, 0))[side]
        return pltpu.make_async_remote_copy(
            fields[n].at[p + 1, here], fields[n].at[p + 1, there],
            row_send.at[n, side, p], row_recv.at[n, side, p],
            device_id=(up, down)[side], device_id_type=MESH,
        )

    def col_copy(n, p, side):
        return pltpu.make_async_remote_copy(
            edge_out.at[n, side, p], edge_in.at[n, side, p],
            col_send.at[n, side, p], col_recv.at[n, side, p],
            device_id=(left, right)[side], device_id_type=MESH,
        )

    def send_rows(n, p):
        for side in range(2):
            row_copy(n, p, side).start()

    def send_edges(n, p, left_edge, right_edge):
        edge_out[n, 0, p] = left_edge
        edge_out[n, 1, p] = right_edge
        for side in range(2):
            col_copy(n, p, side).start()

    def load(p, i):
        return pltpu.make_async_copy(bits.at[i, p], raw.at[p, :, i, :], load_sem.at[p, i])

    barrier = pltpu.get_barrier_semaphore()
    for d in range(1, GXN):
        pl.semaphore_signal(barrier, inc=1, device_id=(lax.rem(gx + d, GXN), gy), device_id_type=MESH)
    for d in range(1, GYN):
        pl.semaphore_signal(barrier, inc=1, device_id=(gx, lax.rem(gy + d, GYN)), device_id_type=MESH)

    @pl.loop(0, PL)
    def _(p):
        for i in range(PROBES):
            load(p, i).start()

    lev_copy = pltpu.make_async_copy(levels, lev, lev_sem)
    lev_copy.start()

    source = lax.broadcasted_iota(jnp.int32, (BLOCK, BLOCK), 0)
    place = lax.broadcasted_iota(jnp.int32, (BLOCK, BLOCK), 1)
    mix[...] = jnp.where(source == lax.rem(place, 128) * 2 + place // 128, 1.0, 0.0).astype(BF16)
    unmix[...] = jnp.where(place == lax.rem(source, 128) * 2 + source // 128, 1.0, 0.0).astype(BF16)

    def moved(value, matrix):
        order = matrix[...]
        return jnp.concatenate(
            [
                lax.dot_general(
                    value[:, c : c + BLOCK], order, (((1,), (0,)), ((), ())), preferred_element_type=F32
                )
                for c in range(0, COLS, BLOCK)
            ],
            1,
        )

    def begin(p):
        for i in range(PROBES):
            load(p, i).wait()
        signs = (2 * raw[p] - 1).astype(F32).reshape(ROWS * PROBES, COLS)
        value = moved(signs.astype(BF16), mix)
        halves[p, 0 : ROWS * PROBES] = value.astype(BF16)
        left_edge, right_edge = jnp.zeros((8, 128), F32), jnp.zeros((8, 128), F32)
        lane = lanes()
        for x in range(ROWS):
            row = value[x * PROBES : (x + 1) * PROBES]
            field0[p + 1, x + 1] = row
            left_edge = jnp.where(lane == x, pltpu.roll(row[:, 0:128], x, 1), left_edge)
            right_edge = jnp.where(lane == x, pltpu.roll(row[:, COLS - 128 :], x + 1, 1), right_edge)
        return left_edge, right_edge

    pl.semaphore_wait(barrier, GXN + GYN - 2)

    @pl.loop(0, PL)
    def _(p):
        left_edge, right_edge = begin(p)
        send_edges(0, p, left_edge, right_edge)
        if DEFER == 0:
            send_rows(0, p)
        else:
            pl.when(p < PL - DEFER)(lambda: send_rows(0, p))

    for field in fields:
        for p in (0, PL + 1):

            @pl.loop(0, ROWS + 2)
            def _(x):
                field[p, x] = jnp.zeros((PROBES, COLS), F32)

    grams[...] = jnp.zeros_like(grams)

    lev_copy.wait()
    level = moved(lev[...].astype(F32).astype(BF16).reshape(PL * ROWS, COLS), mix)
    for x in range(ROWS):
        slope = field_strength * (((gx * ROWS + x).astype(F32) + 0.5) / NX - 0.5)
        for p in range(PL):
            at = p * ROWS + x
            value = disorder_width * (level[at : at + 1] / (LEVELS - 1) - 0.5) + slope
            onsite[p, x] = jnp.broadcast_to(value, (PROBES, COLS))

    def step(n, p):
        field, base = fields[n], p + 1
        older = fields[n - 1] if n else None
        newer = fields[n + 1] if n + 1 < STEPS else None
        kept, fresh = (n % 2) * HALF, ((n + 1) % 2) * HALF
        for side in range(2):
            col_copy(n, p, side).wait_recv()
            row_copy(n, p, side).wait_recv()
        from_right, from_left = edge_in[n, 0, p], edge_in[n, 1, p]
        left_edge, right_edge = jnp.zeros((8, 128), F32), jnp.zeros((8, 128), F32)
        lane = lanes()
        is_first, is_last = lane == 0, lane == 127

        def tiles(x):
            return [field[base, x, :, t * 128 : (t + 1) * 128] for t in range(TILES)]

        above, now = tiles(0), tiles(1)
        pair = []
        for x in range(ROWS):
            below = tiles(x + 2)
            forth = [pltpu.roll(from_left, (128 - x) % 128, 1)]
            forth += [pltpu.roll(now[t], 1, 1) for t in range(1, TILES, 2)]
            back = [pltpu.roll(now[t], 127, 1) for t in range(0, TILES, 2)]
            back += [pltpu.roll(from_right, 127 - x, 1)]
            around = []
            for t in range(0, TILES, 2):
                around.append(now[t + 1] + jnp.where(is_first, forth[t // 2], forth[t // 2 + 1]))
                around.append(now[t] + jnp.where(is_last, back[t // 2 + 1], back[t // 2]))
            made = []
            for t in range(TILES):
                cut = pl.ds(t * 128, 128)
                beside = (below[t] + above[t]) + around[t]
                beside = beside + (field[base + 1, x + 1, :, cut] + field[base - 1, x + 1, :, cut])
                hopped = onsite[p, x, :, cut] * now[t] - beside
                if n == 0:
                    value = hopped * (1.0 / spectral_scale)
                else:
                    value = hopped * (2.0 / spectral_scale) - older[base, x + 1, :, cut]
                if n + 1 < STEPS:
                    newer[base, x + 1, :, cut] = value
                made.append(value)
            if n + 1 < STEPS:
                left_edge = jnp.where(lane == x, pltpu.roll(made[0], x, 1), left_edge)
                right_edge = jnp.where(lane == x, pltpu.roll(made[TILES - 1], x + 1, 1), right_edge)
            pair.append(made)
            if len(pair) == 2:
                at = (x - 1) * PROBES
                for t in range(TILES):
                    cut = pl.ds(t * 128, 128)
                    high, low = split(jnp.concatenate([pair[0][t], pair[1][t]], 0))
                    halves[p, fresh + at : fresh + at + 16, cut] = high
                    halves[p, fresh + PART + at : fresh + PART + at + 16, cut] = low
                pair = []
            above, now = now, below

        if n + 1 < STEPS:
            send_edges(n + 1, p, left_edge, right_edge)
            if DEFER == 0:
                send_rows(n + 1, p)
            else:
                pl.when(p >= DEFER)(lambda: send_rows(n + 1, p - DEFER))
        if DEFER:
            pl.when(p < DEFER)(lambda: send_rows(n, p + PL - DEFER))

        if n + 1 == STEPS:
            both = moved(halves[p, fresh : fresh + HALF], unmix)
            last[p] = (both[0:PART] + both[PART:HALF]).reshape(ROWS, PROBES, COLS)

        lane_group = lanes() // PROBES
        stays = halves[p, kept : kept + (PART if n == 0 else HALF)]
        own, other = halves[p, kept : kept + PART], halves[p, fresh : fresh + HALF]
        if n % 2 == 0:
            streamed = [(own, (0,)), (other, (0, 1))]
        else:
            streamed = [(halves[p, 0 : HALF + PART], (0, 1, 2))]
        blocks = []
        for left_rows, parts in streamed:
            product = lax.dot_general(left_rows, stays, (((1,), (1,)), ((), ())), preferred_element_type=F32)
            blocks += [product[q * PART : (q + 1) * PART] for q in parts]
        if n % 2:
            blocks = [blocks[2], blocks[0], blocks[1]]

        def equal_rows(block, c):
            chosen = block[0:PROBES, c : c + 128]
            for x in range(1, ROWS):
                chosen = jnp.where(lane_group == x, block[x * PROBES : (x + 1) * PROBES, c : c + 128], chosen)
            return chosen

        grams[n, 0] += equal_rows(blocks[0], 0)
        crossed = equal_rows(blocks[1], 0) + equal_rows(blocks[2], 0)
        if n:
            grams[n, 1] += equal_rows(blocks[0], PART)
            crossed = crossed + equal_rows(blocks[1], PART) + equal_rows(blocks[2], PART)
        grams[n, 2] += crossed

    sub = lax.broadcasted_iota(jnp.int32, (8, 128), 0)
    keep = sub == lanes() // PROBES

    def over_rows(total):
        for shift in (8, 16, 32, 64):
            total = total + pltpu.roll(total, shift, 1)
        return total

    def turned(total):
        return jnp.transpose(jnp.concatenate([total] * ROWS, 0))[0:PROBES]

    packed = jnp.zeros((8, 128), F32)
    for n in range(STEPS):
        pl.loop(0, PL)(functools.partial(step, n))
        even, odd = over_rows(grams[n, 0]), turned(over_rows(grams[n, 2]))
        if n:
            low = over_rows(grams[n, 1])
            even = even + low + turned(low)
        for m, total in ((2 * n, even), (2 * n + 1, odd)):
            row = jnp.sum(jnp.where(keep, total, 0.0), axis=0, keepdims=True)
            packed = jnp.where(sub == m, jnp.broadcast_to(row, (8, 128)), packed)
    flat[...] = packed

    first[gy] = packed
    copies = []
    for d in range(1, GYN):
        c = pltpu.make_async_remote_copy(
            flat, first.at[gy], sum_send.at[0, d], sum_recv.at[0, d],
            device_id=(gx, lax.rem(gy + d, GYN)), device_id_type=MESH,
        )
        c.start()
        copies.append(c)
    for d in range(1, GYN):
        pltpu.make_async_remote_copy(
            flat, first.at[lax.rem(gy + GYN - d, GYN)], sum_send.at[0, d], sum_recv.at[0, d],
            device_id=(gx, lax.rem(gy + d, GYN)), device_id_type=MESH,
        ).wait_recv()
    total = first[0]
    for d in range(1, GYN):
        total = total + first[d]
    second[gx] = total
    for d in range(1, GXN):
        c = pltpu.make_async_remote_copy(
            second.at[gx], second.at[gx], sum_send.at[1, d], sum_recv.at[1, d],
            device_id=(lax.rem(gx + d, GXN), gy), device_id_type=MESH,
        )
        c.start()
        copies.append(c)
    for d in range(1, GXN):
        source = lax.rem(gx + GXN - d, GXN)
        pltpu.make_async_remote_copy(
            second.at[source], second.at[source], sum_send.at[1, d], sum_recv.at[1, d],
            device_id=(lax.rem(gx + d, GXN), gy), device_id_type=MESH,
        ).wait_recv()
    total = second[0]
    for d in range(1, GXN):
        total = total + second[d]
    moments_out[...] = total

    for c in copies:
        c.wait_send()
    for n in range(STEPS):

        @pl.loop(0, PL)
        def _(p):
            for side in range(2):
                row_copy(n, p, side).wait_send()
                col_copy(n, p, side).wait_send()


def finish_kernel(vector, grams, table, green, out, table_here, out_sem, table_sem):
    device = lax.axis_index("gx") * GYN + lax.axis_index("gy")
    fetch = pltpu.make_async_copy(table.at[device], table_here, table_sem)
    fetch.start()
    copies = []
    for p in range(PL):
        for i in range(PROBES):
            c = pltpu.make_async_copy(vector.at[p, :, i, :], out.at[i, p], out_sem.at[p, i])
            c.start()
            copies.append(c)
    fetch.wait()
    scaled = grams[...] / SITES
    rows = [scaled[0:1], scaled[1:2]]
    for m in range(2, NMOM):
        rows.append(2.0 * scaled[m : m + 1] - rows[m % 2])
    moments = jnp.concatenate(rows + [jnp.zeros((128 - NMOM, 128), F32)], 0)
    weights = jnp.transpose(jnp.concatenate([table_here[...], jnp.zeros((128 - NMOM, 128), F32)], 0))
    result = jnp.dot(weights, moments, precision=lax.Precision.HIGHEST, preferred_element_type=F32)
    green[0] = result[0:EB, 0 : PROBES * PROBES]
    green[1] = result[EB : 2 * EB, 0 : PROBES * PROBES]
    for c in copies:
        c.wait()


def on_device(levels, probe_bits):
    anywhere = pl.BlockSpec(memory_space=pl.ANY)
    vmem = pl.BlockSpec(memory_space=pltpu.VMEM)
    dma = pltpu.SemaphoreType.DMA
    last, grams = pl.pallas_call(
        main_kernel,
        out_shape=(
            pltpu.VMEM((PL, ROWS, PROBES, COLS), F32),
            pltpu.VMEM((8, 128), F32),
        ),
        in_specs=[anywhere, anywhere],
        out_specs=(vmem, vmem),
        scratch_shapes=[
            pltpu.VMEM((PL + 2, ROWS + 2, PROBES, COLS), F32),
            pltpu.VMEM((PL + 2, ROWS + 2, PROBES, COLS), F32),
            pltpu.VMEM((PL + 2, ROWS + 2, PROBES, COLS), F32),
            pltpu.VMEM((PL + 2, ROWS + 2, PROBES, COLS), F32),
            pltpu.VMEM((PL, ROWS, PROBES, COLS), jnp.int32),
            pltpu.VMEM((PL, 2 * HALF, COLS), BF16),
            pltpu.VMEM((PL, ROWS, PROBES, COLS), F32),
            pltpu.VMEM((PL, ROWS, COLS), jnp.int32),
            pltpu.VMEM((BLOCK, BLOCK), BF16),
            pltpu.VMEM((BLOCK, BLOCK), BF16),
            pltpu.VMEM((STEPS, 2, PL, 8, 128), F32),
            pltpu.VMEM((STEPS, 2, PL, 8, 128), F32),
            pltpu.VMEM((STEPS, 3, 8, 128), F32),
            pltpu.VMEM((8, 128), F32),
            pltpu.VMEM((GYN, 8, 128), F32),
            pltpu.VMEM((GXN, 8, 128), F32),
            dma((STEPS, 2, PL)),
            dma((STEPS, 2, PL)),
            dma((STEPS, 2, PL)),
            dma((STEPS, 2, PL)),
            dma((PL, PROBES)),
            dma,
            dma((2, GYN)),
            dma((2, GYN)),
        ],
        compiler_params=pltpu.CompilerParams(
            collective_id=0, has_side_effects=True, vmem_limit_bytes=54 << 20
        ),
    )(levels, probe_bits)
    green, out = pl.pallas_call(
        finish_kernel,
        out_shape=(
            jax.ShapeDtypeStruct((2, EB, PROBES * PROBES), F32),
            jax.ShapeDtypeStruct((PROBES, PL, ROWS, COLS), F32),
        ),
        in_specs=[vmem, vmem, anywhere],
        out_specs=(vmem, anywhere),
        scratch_shapes=[
            pltpu.VMEM((NMOM, 2 * EB), F32),
            dma((PL, PROBES)),
            dma,
        ],
        compiler_params=pltpu.CompilerParams(vmem_limit_bytes=8 << 20),
    )(last, grams, jnp.asarray(energy_tables()))
    return green, out


def solution(mesh):
    return jax.shard_map(
        on_device,
        mesh=mesh,
        in_specs=(P(None, "gx", "gy"), P(None, None, "gx", "gy")),
        out_specs=(P(None, ("gx", "gy"), None), P(None, None, "gx", "gy")),
        check_vma=False,
    )
```

```python
import functools
import math

import jax
import jax.numpy as jnp
import numpy as np
from jax import lax
from jax.experimental import pallas as pl
from jax.experimental.pallas import tpu as pltpu
from jax.sharding import PartitionSpec as P

PROBES = 8
PL = 8
STEPS = 4
LEVELS = 8
NE = 8192
NMOM = 8
NX = 128
NY = 16384
SITES = 16777216
GXN = 8
GYN = 16
ROWS = NX // GXN
COLS = NY // GYN
TILES = COLS // 128
EB = NE // (GXN * GYN)
DEFER = 3
PART = ROWS * PROBES
HALF = 2 * PART
BLOCK = 256

disorder_width = 4.0
field_strength = 3.0
spectral_scale = 10.0
energy_edge = 0.9

MESH = pl.DeviceIdType.MESH
F32 = jnp.float32
BF16 = jnp.bfloat16


def energy_tables():
    theta = np.arccos(energy_edge * np.cos(math.pi * (np.arange(NE) + 0.5) / NE))
    total = NMOM + 1.0
    rows = []
    for m in range(NMOM):
        damp = (
            (NMOM - m + 1.0) * math.cos(math.pi * m / total)
            + math.sin(math.pi * m / total) / math.tan(math.pi / total)
        ) / total
        weight = damp if m == 0 else 2.0 * damp
        rows.append(
            np.stack(
                [
                    -weight * np.sin(m * theta) / np.sin(theta),
                    -weight * np.cos(m * theta) / np.sin(theta),
                ]
            )
        )
    table = np.stack(rows).reshape(NMOM, 2, GXN * GYN, EB)
    return np.ascontiguousarray(table.transpose(2, 0, 1, 3).reshape(GXN * GYN, NMOM, 2 * EB)).astype(np.float32)


def lanes():
    return lax.broadcasted_iota(jnp.int32, (8, 128), 1)


def split(pair):
    high = pair.astype(BF16)
    return high, (pair - high.astype(F32)).astype(BF16)


def main_kernel(
    levels, bits, last, moments_out,
    field0, field1, field2, field3, raw, halves, onsite, lev, mix, unmix,
    edge_out, edge_in, grams, flat, first, second,
    row_send, row_recv, col_send, col_recv, load_sem, lev_sem, sum_send, sum_recv,
):
    fields = (field0, field1, field2, field3)
    gx, gy = lax.axis_index("gx"), lax.axis_index("gy")
    up, down = (lax.rem(gx + GXN - 1, GXN), gy), (lax.rem(gx + 1, GXN), gy)
    left, right = (gx, lax.rem(gy + GYN - 1, GYN)), (gx, lax.rem(gy + 1, GYN))

    def row_copy(n, p, side):
        here, there = ((1, ROWS + 1), (ROWS, 0))[side]
        return pltpu.make_async_remote_copy(
            fields[n].at[p + 1, here], fields[n].at[p + 1, there],
            row_send.at[n, side, p], row_recv.at[n, side, p],
            device_id=(up, down)[side], device_id_type=MESH,
        )

    def col_copy(n, p, side):
        return pltpu.make_async_remote_copy(
            edge_out.at[n, side, p], edge_in.at[n, side, p],
            col_send.at[n, side, p], col_recv.at[n, side, p],
            device_id=(left, right)[side], device_id_type=MESH,
        )

    def send_rows(n, p):
        for side in range(2):
            row_copy(n, p, side).start()

    def send_edges(n, p, left_edge, right_edge):
        edge_out[n, 0, p] = left_edge
        edge_out[n, 1, p] = right_edge
        for side in range(2):
            col_copy(n, p, side).start()

    def load(p, i):
        return pltpu.make_async_copy(bits.at[i, p], raw.at[p, :, i, :], load_sem.at[p, i])

    barrier = pltpu.get_barrier_semaphore()
    for d in range(1, GXN):
        pl.semaphore_signal(barrier, inc=1, device_id=(lax.rem(gx + d, GXN), gy), device_id_type=MESH)
    for d in range(1, GYN):
        pl.semaphore_signal(barrier, inc=1, device_id=(gx, lax.rem(gy + d, GYN)), device_id_type=MESH)

    lev_copy = pltpu.make_async_copy(levels, lev, lev_sem)
    lev_copy.start()

    @pl.loop(0, PL)
    def _(p):
        for i in range(PROBES):
            load(p, i).start()

    source = lax.broadcasted_iota(jnp.int32, (BLOCK, BLOCK), 0)
    place = lax.broadcasted_iota(jnp.int32, (BLOCK, BLOCK), 1)
    mix[...] = jnp.where(source == lax.rem(place, 128) * 2 + place // 128, 1.0, 0.0).astype(BF16)
    unmix[...] = jnp.where(place == lax.rem(source, 128) * 2 + source // 128, 1.0, 0.0).astype(BF16)

    def moved(value, matrix):
        order = matrix[...]
        return jnp.concatenate(
            [
                lax.dot_general(
                    value[:, c : c + BLOCK], order, (((1,), (0,)), ((), ())), preferred_element_type=F32
                )
                for c in range(0, COLS, BLOCK)
            ],
            1,
        )

    def begin(p):
        for i in range(PROBES):
            load(p, i).wait()
        signs = (2 * raw[p] - 1).astype(F32).reshape(ROWS * PROBES, COLS)
        value = moved(signs.astype(BF16), mix)
        halves[p, 0 : ROWS * PROBES] = value.astype(BF16)
        left_edge, right_edge = jnp.zeros((8, 128), F32), jnp.zeros((8, 128), F32)
        lane = lanes()
        for x in range(ROWS):
            row = value[x * PROBES : (x + 1) * PROBES]
            field0[p + 1, x + 1] = row
            left_edge = jnp.where(lane == x, pltpu.roll(row[:, 0:128], x, 1), left_edge)
            right_edge = jnp.where(lane == x, pltpu.roll(row[:, COLS - 128 :], x + 1, 1), right_edge)
        return left_edge, right_edge

    for field in fields:
        for p in (0, PL + 1):

            @pl.loop(0, ROWS + 2)
            def _(x):
                field[p, x] = jnp.zeros((PROBES, COLS), F32)

    grams[...] = jnp.zeros_like(grams)

    lev_copy.wait()
    level = moved(lev[...].astype(F32).astype(BF16).reshape(PL * ROWS, COLS), mix)
    for x in range(ROWS):
        slope = field_strength * (((gx * ROWS + x).astype(F32) + 0.5) / NX - 0.5)
        for p in range(PL):
            at = p * ROWS + x
            value = disorder_width * (level[at : at + 1] / (LEVELS - 1) - 0.5) + slope
            onsite[p, x] = jnp.broadcast_to(value, (PROBES, COLS))

    pl.semaphore_wait(barrier, GXN + GYN - 2)

    @pl.loop(0, PL // 2)
    def _(q):
        send_edges(0, 2 * q, *begin(2 * q))
        send_rows(0, q)
        send_edges(0, 2 * q + 1, *begin(2 * q + 1))

    for p in range(PL // 2, PL - DEFER):
        send_rows(0, p)

    def step(n, p):
        field, base = fields[n], p + 1
        older = fields[n - 1] if n else None
        newer = fields[n + 1] if n + 1 < STEPS else None
        kept, fresh = (n % 2) * HALF, ((n + 1) % 2) * HALF
        for side in range(2):
            col_copy(n, p, side).wait_recv()
            row_copy(n, p, side).wait_recv()
        from_right, from_left = edge_in[n, 0, p], edge_in[n, 1, p]
        left_edge, right_edge = jnp.zeros((8, 128), F32), jnp.zeros((8, 128), F32)
        lane = lanes()
        is_first, is_last = lane == 0, lane == 127

        def tiles(x):
            return [field[base, x, :, t * 128 : (t + 1) * 128] for t in range(TILES)]

        above, now = tiles(0), tiles(1)
        pair = []
        for x in range(ROWS):
            below = tiles(x + 2)
            forth = [pltpu.roll(from_left, (128 - x) % 128, 1)]
            forth += [pltpu.roll(now[t], 1, 1) for t in range(1, TILES, 2)]
            back = [pltpu.roll(now[t], 127, 1) for t in range(0, TILES, 2)]
            back += [pltpu.roll(from_right, 127 - x, 1)]
            around = []
            for t in range(0, TILES, 2):
                around.append(now[t + 1] + jnp.where(is_first, forth[t // 2], forth[t // 2 + 1]))
                around.append(now[t] + jnp.where(is_last, back[t // 2 + 1], back[t // 2]))
            made = []
            for t in range(TILES):
                cut = pl.ds(t * 128, 128)
                beside = (below[t] + above[t]) + around[t]
                beside = beside + (field[base + 1, x + 1, :, cut] + field[base - 1, x + 1, :, cut])
                hopped = onsite[p, x, :, cut] * now[t] - beside
                if n == 0:
                    value = hopped * (1.0 / spectral_scale)
                else:
                    value = hopped * (2.0 / spectral_scale) - older[base, x + 1, :, cut]
                if n + 1 < STEPS:
                    newer[base, x + 1, :, cut] = value
                made.append(value)
            if n + 1 < STEPS:
                left_edge = jnp.where(lane == x, pltpu.roll(made[0], x, 1), left_edge)
                right_edge = jnp.where(lane == x, pltpu.roll(made[TILES - 1], x + 1, 1), right_edge)
            pair.append(made)
            if len(pair) == 2:
                at = (x - 1) * PROBES
                for t in range(TILES):
                    cut = pl.ds(t * 128, 128)
                    high, low = split(jnp.concatenate([pair[0][t], pair[1][t]], 0))
                    halves[p, fresh + at : fresh + at + 16, cut] = high
                    halves[p, fresh + PART + at : fresh + PART + at + 16, cut] = low
                pair = []
            above, now = now, below

        if n + 1 < STEPS:
            send_edges(n + 1, p, left_edge, right_edge)
            if DEFER == 0:
                send_rows(n + 1, p)
            else:
                pl.when(p >= DEFER)(lambda: send_rows(n + 1, p - DEFER))
        if DEFER:
            pl.when(p < DEFER)(lambda: send_rows(n, p + PL - DEFER))

        if n + 1 == STEPS:
            both = moved(halves[p, fresh : fresh + HALF], unmix)
            last[p] = (both[0:PART] + both[PART:HALF]).reshape(ROWS, PROBES, COLS)

        lane_group = lanes() // PROBES
        stays = halves[p, kept : kept + (PART if n == 0 else HALF)]
        own, other = halves[p, kept : kept + PART], halves[p, fresh : fresh + HALF]
        if n % 2 == 0:
            streamed = [(own, (0,)), (other, (0, 1))]
        else:
            streamed = [(halves[p, 0 : HALF + PART], (0, 1, 2))]
        blocks = []
        for left_rows, parts in streamed:
            product = lax.dot_general(left_rows, stays, (((1,), (1,)), ((), ())), preferred_element_type=F32)
            blocks += [product[q * PART : (q + 1) * PART] for q in parts]
        if n % 2:
            blocks = [blocks[2], blocks[0], blocks[1]]

        def equal_rows(block, c):
            chosen = block[0:PROBES, c : c + 128]
            for x in range(1, ROWS):
                chosen = jnp.where(lane_group == x, block[x * PROBES : (x + 1) * PROBES, c : c + 128], chosen)
            return chosen

        grams[n, 0] += equal_rows(blocks[0], 0)
        crossed = equal_rows(blocks[1], 0) + equal_rows(blocks[2], 0)
        if n:
            grams[n, 1] += equal_rows(blocks[0], PART)
            crossed = crossed + equal_rows(blocks[1], PART) + equal_rows(blocks[2], PART)
        grams[n, 2] += crossed

    sub = lax.broadcasted_iota(jnp.int32, (8, 128), 0)
    keep = sub == lanes() // PROBES

    def over_rows(total):
        for shift in (8, 16, 32, 64):
            total = total + pltpu.roll(total, shift, 1)
        return total

    def turned(total):
        return jnp.transpose(jnp.concatenate([total] * ROWS, 0))[0:PROBES]

    packed = jnp.zeros((8, 128), F32)
    for n in range(STEPS):
        pl.loop(0, PL)(functools.partial(step, n))
        even, odd = over_rows(grams[n, 0]), turned(over_rows(grams[n, 2]))
        if n:
            low = over_rows(grams[n, 1])
            even = even + low + turned(low)
        for m, total in ((2 * n, even), (2 * n + 1, odd)):
            row = jnp.sum(jnp.where(keep, total, 0.0), axis=0, keepdims=True)
            packed = jnp.where(sub == m, jnp.broadcast_to(row, (8, 128)), packed)
    flat[...] = packed

    first[gy] = packed
    copies = []
    for d in range(1, GYN):
        c = pltpu.make_async_remote_copy(
            flat, first.at[gy], sum_send.at[0, d], sum_recv.at[0, d],
            device_id=(gx, lax.rem(gy + d, GYN)), device_id_type=MESH,
        )
        c.start()
        copies.append(c)
    for d in range(1, GYN):
        pltpu.make_async_remote_copy(
            flat, first.at[lax.rem(gy + GYN - d, GYN)], sum_send.at[0, d], sum_recv.at[0, d],
            device_id=(gx, lax.rem(gy + d, GYN)), device_id_type=MESH,
        ).wait_recv()
    total = first[0]
    for d in range(1, GYN):
        total = total + first[d]
    second[gx] = total
    for d in range(1, GXN):
        c = pltpu.make_async_remote_copy(
            second.at[gx], second.at[gx], sum_send.at[1, d], sum_recv.at[1, d],
            device_id=(lax.rem(gx + d, GXN), gy), device_id_type=MESH,
        )
        c.start()
        copies.append(c)
    for d in range(1, GXN):
        source = lax.rem(gx + GXN - d, GXN)
        pltpu.make_async_remote_copy(
            second.at[source], second.at[source], sum_send.at[1, d], sum_recv.at[1, d],
            device_id=(lax.rem(gx + d, GXN), gy), device_id_type=MESH,
        ).wait_recv()
    total = second[0]
    for d in range(1, GXN):
        total = total + second[d]
    moments_out[...] = total

    for c in copies:
        c.wait_send()
    for n in range(STEPS):

        @pl.loop(0, PL)
        def _(p):
            for side in range(2):
                row_copy(n, p, side).wait_send()
                col_copy(n, p, side).wait_send()


def finish_kernel(vector, grams, table, green, out, table_here, out_sem, table_sem):
    device = lax.axis_index("gx") * GYN + lax.axis_index("gy")
    fetch = pltpu.make_async_copy(table.at[device], table_here, table_sem)
    fetch.start()
    copies = []
    for p in range(PL):
        for i in range(PROBES):
            c = pltpu.make_async_copy(vector.at[p, :, i, :], out.at[i, p], out_sem.at[p, i])
            c.start()
            copies.append(c)
    fetch.wait()
    scaled = grams[...] / SITES
    rows = [scaled[0:1], scaled[1:2]]
    for m in range(2, NMOM):
        rows.append(2.0 * scaled[m : m + 1] - rows[m % 2])
    moments = jnp.concatenate(rows + [jnp.zeros((128 - NMOM, 128), F32)], 0)
    weights = jnp.transpose(jnp.concatenate([table_here[...], jnp.zeros((128 - NMOM, 128), F32)], 0))
    result = jnp.dot(weights, moments, precision=lax.Precision.HIGHEST, preferred_element_type=F32)
    green[0] = result[0:EB, 0 : PROBES * PROBES]
    green[1] = result[EB : 2 * EB, 0 : PROBES * PROBES]
    for c in copies:
        c.wait()


def on_device(levels, probe_bits):
    anywhere = pl.BlockSpec(memory_space=pl.ANY)
    vmem = pl.BlockSpec(memory_space=pltpu.VMEM)
    dma = pltpu.SemaphoreType.DMA
    last, grams = pl.pallas_call(
        main_kernel,
        out_shape=(
            pltpu.VMEM((PL, ROWS, PROBES, COLS), F32),
            pltpu.VMEM((8, 128), F32),
        ),
        in_specs=[anywhere, anywhere],
        out_specs=(vmem, vmem),
        scratch_shapes=[
            pltpu.VMEM((PL + 2, ROWS + 2, PROBES, COLS), F32),
            pltpu.VMEM((PL + 2, ROWS + 2, PROBES, COLS), F32),
            pltpu.VMEM((PL + 2, ROWS + 2, PROBES, COLS), F32),
            pltpu.VMEM((PL + 2, ROWS + 2, PROBES, COLS), F32),
            pltpu.VMEM((PL, ROWS, PROBES, COLS), jnp.int32),
            pltpu.VMEM((PL, 2 * HALF, COLS), BF16),
            pltpu.VMEM((PL, ROWS, PROBES, COLS), F32),
            pltpu.VMEM((PL, ROWS, COLS), jnp.int32),
            pltpu.VMEM((BLOCK, BLOCK), BF16),
            pltpu.VMEM((BLOCK, BLOCK), BF16),
            pltpu.VMEM((STEPS, 2, PL, 8, 128), F32),
            pltpu.VMEM((STEPS, 2, PL, 8, 128), F32),
            pltpu.VMEM((STEPS, 3, 8, 128), F32),
            pltpu.VMEM((8, 128), F32),
            pltpu.VMEM((GYN, 8, 128), F32),
            pltpu.VMEM((GXN, 8, 128), F32),
            dma((STEPS, 2, PL)),
            dma((STEPS, 2, PL)),
            dma((STEPS, 2, PL)),
            dma((STEPS, 2, PL)),
            dma((PL, PROBES)),
            dma,
            dma((2, GYN)),
            dma((2, GYN)),
        ],
        compiler_params=pltpu.CompilerParams(
            collective_id=0, has_side_effects=True, vmem_limit_bytes=54 << 20
        ),
    )(levels, probe_bits)
    green, out = pl.pallas_call(
        finish_kernel,
        out_shape=(
            jax.ShapeDtypeStruct((2, EB, PROBES * PROBES), F32),
            jax.ShapeDtypeStruct((PROBES, PL, ROWS, COLS), F32),
        ),
        in_specs=[vmem, vmem, anywhere],
        out_specs=(vmem, anywhere),
        scratch_shapes=[
            pltpu.VMEM((NMOM, 2 * EB), F32),
            dma((PL, PROBES)),
            dma,
        ],
        compiler_params=pltpu.CompilerParams(vmem_limit_bytes=8 << 20),
    )(last, grams, jnp.asarray(energy_tables()))
    return green, out


def solution(mesh):
    return jax.shard_map(
        on_device,
        mesh=mesh,
        in_specs=(P(None, "gx", "gy"), P(None, None, "gx", "gy")),
        out_specs=(P(None, ("gx", "gy"), None), P(None, None, "gx", "gy")),
        check_vma=False,
    )
```

```python
import functools
import math

import jax
import jax.numpy as jnp
import numpy as np
from jax import lax
from jax.experimental import pallas as pl
from jax.experimental.pallas import tpu as pltpu
from jax.sharding import PartitionSpec as P

PROBES = 8
PL = 8
STEPS = 4
LEVELS = 8
NE = 8192
NMOM = 8
NX = 128
NY = 16384
SITES = 16777216
GXN = 8
GYN = 16
ROWS = NX // GXN
COLS = NY // GYN
TILES = COLS // 128
EB = NE // (GXN * GYN)
DEFER = 3
PART = ROWS * PROBES
HALF = 2 * PART
BLOCK = 256

disorder_width = 4.0
field_strength = 3.0
spectral_scale = 10.0
energy_edge = 0.9

MESH = pl.DeviceIdType.MESH
F32 = jnp.float32
BF16 = jnp.bfloat16


def energy_tables():
    theta = np.arccos(energy_edge * np.cos(math.pi * (np.arange(NE) + 0.5) / NE))
    total = NMOM + 1.0
    rows = []
    for m in range(NMOM):
        damp = (
            (NMOM - m + 1.0) * math.cos(math.pi * m / total)
            + math.sin(math.pi * m / total) / math.tan(math.pi / total)
        ) / total
        weight = damp if m == 0 else 2.0 * damp
        rows.append(
            np.stack(
                [
                    -weight * np.sin(m * theta) / np.sin(theta),
                    -weight * np.cos(m * theta) / np.sin(theta),
                ]
            )
        )
    table = np.stack(rows).reshape(NMOM, 2, GXN * GYN, EB)
    return np.ascontiguousarray(table.transpose(2, 0, 1, 3).reshape(GXN * GYN, NMOM, 2 * EB)).astype(np.float32)


def lanes():
    return lax.broadcasted_iota(jnp.int32, (8, 128), 1)


def split(pair):
    high = pair.astype(BF16)
    return high, (pair - high.astype(F32)).astype(BF16)


def main_kernel(
    levels, bits, last, moments_out,
    field0, field1, field2, field3, raw, halves, onsite, lev, mix, unmix,
    edge_out, edge_in, grams, flat, first, second,
    row_send, row_recv, col_send, col_recv, load_sem, lev_sem, sum_send, sum_recv,
):
    fields = (field0, field1, field2, field3)
    gx, gy = lax.axis_index("gx"), lax.axis_index("gy")
    up, down = (lax.rem(gx + GXN - 1, GXN), gy), (lax.rem(gx + 1, GXN), gy)
    left, right = (gx, lax.rem(gy + GYN - 1, GYN)), (gx, lax.rem(gy + 1, GYN))

    def row_copy(n, p, side):
        here, there = ((1, ROWS + 1), (ROWS, 0))[side]
        return pltpu.make_async_remote_copy(
            fields[n].at[p + 1, here], fields[n].at[p + 1, there],
            row_send.at[n, side, p], row_recv.at[n, side, p],
            device_id=(up, down)[side], device_id_type=MESH,
        )

    def col_copy(n, p, side):
        return pltpu.make_async_remote_copy(
            edge_out.at[n, side, p], edge_in.at[n, side, p],
            col_send.at[n, side, p], col_recv.at[n, side, p],
            device_id=(left, right)[side], device_id_type=MESH,
        )

    def send_rows(n, p):
        for side in range(2):
            row_copy(n, p, side).start()

    def send_edges(n, p, left_edge, right_edge):
        edge_out[n, 0, p] = left_edge
        edge_out[n, 1, p] = right_edge
        for side in range(2):
            col_copy(n, p, side).start()

    def load(p, i):
        return pltpu.make_async_copy(bits.at[i, p], raw.at[p, :, i, :], load_sem.at[p, i])

    barrier = pltpu.get_barrier_semaphore()
    for d in range(1, GXN):
        pl.semaphore_signal(barrier, inc=1, device_id=(lax.rem(gx + d, GXN), gy), device_id_type=MESH)
    for d in range(1, GYN):
        pl.semaphore_signal(barrier, inc=1, device_id=(gx, lax.rem(gy + d, GYN)), device_id_type=MESH)

    lev_copy = pltpu.make_async_copy(levels, lev, lev_sem)
    lev_copy.start()

    @pl.loop(0, PL)
    def _(p):
        for i in range(PROBES):
            load(p, i).start()

    source = lax.broadcasted_iota(jnp.int32, (BLOCK, BLOCK), 0)
    place = lax.broadcasted_iota(jnp.int32, (BLOCK, BLOCK), 1)
    mix[...] = jnp.where(source == lax.rem(place, 128) * 2 + place // 128, 1.0, 0.0).astype(BF16)
    unmix[...] = jnp.where(place == lax.rem(source, 128) * 2 + source // 128, 1.0, 0.0).astype(BF16)

    def moved(value, matrix):
        order = matrix[...]
        return jnp.concatenate(
            [
                lax.dot_general(
                    value[:, c : c + BLOCK], order, (((1,), (0,)), ((), ())), preferred_element_type=F32
                )
                for c in range(0, COLS, BLOCK)
            ],
            1,
        )

    def begin(p):
        for i in range(PROBES):
            load(p, i).wait()
        signs = (2 * raw[p] - 1).astype(F32).reshape(ROWS * PROBES, COLS)
        value = moved(signs.astype(BF16), mix)
        halves[p, 0 : ROWS * PROBES] = value.astype(BF16)
        left_edge, right_edge = jnp.zeros((8, 128), F32), jnp.zeros((8, 128), F32)
        lane = lanes()
        for x in range(ROWS):
            row = value[x * PROBES : (x + 1) * PROBES]
            field0[p + 1, x + 1] = row
            left_edge = jnp.where(lane == x, pltpu.roll(row[:, 0:128], x, 1), left_edge)
            right_edge = jnp.where(lane == x, pltpu.roll(row[:, COLS - 128 :], x + 1, 1), right_edge)
        return left_edge, right_edge

    for field in fields:
        for p in (0, PL + 1):

            @pl.loop(0, ROWS + 2)
            def _(x):
                field[p, x] = jnp.zeros((PROBES, COLS), F32)

    grams[...] = jnp.zeros_like(grams)

    lev_copy.wait()
    level = moved(lev[...].astype(F32).astype(BF16).reshape(PL * ROWS, COLS), mix)
    for x in range(ROWS):
        slope = field_strength * (((gx * ROWS + x).astype(F32) + 0.5) / NX - 0.5)
        for p in range(PL):
            at = p * ROWS + x
            value = disorder_width * (level[at : at + 1] / (LEVELS - 1) - 0.5) + slope
            onsite[p, x] = jnp.broadcast_to(value, (PROBES, COLS))

    pl.semaphore_wait(barrier, GXN + GYN - 2)

    @pl.loop(0, PL // 2)
    def _(q):
        send_edges(0, 2 * q, *begin(2 * q))
        send_rows(0, q)
        send_edges(0, 2 * q + 1, *begin(2 * q + 1))

    for p in range(PL // 2, PL - DEFER):
        send_rows(0, p)

    def step(n, p):
        field, base = fields[n], p + 1
        older = fields[n - 1] if n else None
        newer = fields[n + 1] if n + 1 < STEPS else None
        kept, fresh = (n % 2) * HALF, ((n + 1) % 2) * HALF
        for side in range(2):
            col_copy(n, p, side).wait_recv()
            row_copy(n, p, side).wait_recv()
        from_right, from_left = edge_in[n, 0, p], edge_in[n, 1, p]
        left_edge, right_edge = jnp.zeros((8, 128), F32), jnp.zeros((8, 128), F32)
        lane = lanes()
        is_first, is_last = lane == 0, lane == 127

        def tiles(x):
            return [field[base, x, :, t * 128 : (t + 1) * 128] for t in range(TILES)]

        above, now = tiles(0), tiles(1)
        pair = []
        for x in range(ROWS):
            below = tiles(x + 2)
            forth = [pltpu.roll(from_left, (128 - x) % 128, 1)]
            forth += [pltpu.roll(now[t], 1, 1) for t in range(1, TILES, 2)]
            back = [pltpu.roll(now[t], 127, 1) for t in range(0, TILES, 2)]
            back += [pltpu.roll(from_right, 127 - x, 1)]
            around = []
            for t in range(0, TILES, 2):
                around.append(now[t + 1] + jnp.where(is_first, forth[t // 2], forth[t // 2 + 1]))
                around.append(now[t] + jnp.where(is_last, back[t // 2 + 1], back[t // 2]))
            made = []
            for t in range(TILES):
                cut = pl.ds(t * 128, 128)
                beside = (below[t] + above[t]) + around[t]
                beside = beside + (field[base + 1, x + 1, :, cut] + field[base - 1, x + 1, :, cut])
                hopped = onsite[p, x, :, cut] * now[t] - beside
                if n == 0:
                    value = hopped * (1.0 / spectral_scale)
                else:
                    value = hopped * (2.0 / spectral_scale) - older[base, x + 1, :, cut]
                if n + 1 < STEPS:
                    newer[base, x + 1, :, cut] = value
                made.append(value)
            if n + 1 < STEPS:
                left_edge = jnp.where(lane == x, pltpu.roll(made[0], x, 1), left_edge)
                right_edge = jnp.where(lane == x, pltpu.roll(made[TILES - 1], x + 1, 1), right_edge)
            pair.append(made)
            if len(pair) == 2:
                at = (x - 1) * PROBES
                for t in range(TILES):
                    cut = pl.ds(t * 128, 128)
                    high, low = split(jnp.concatenate([pair[0][t], pair[1][t]], 0))
                    halves[p, fresh + at : fresh + at + 16, cut] = high
                    halves[p, fresh + PART + at : fresh + PART + at + 16, cut] = low
                pair = []
            above, now = now, below

        if n + 1 < STEPS:
            send_edges(n + 1, p, left_edge, right_edge)
            if DEFER == 0:
                send_rows(n + 1, p)
            else:
                pl.when(p >= DEFER)(lambda: send_rows(n + 1, p - DEFER))
        if DEFER:
            pl.when(p < DEFER)(lambda: send_rows(n, p + PL - DEFER))

        if n + 1 == STEPS:
            both = moved(halves[p, fresh : fresh + HALF], unmix)
            last[p] = (both[0:PART] + both[PART:HALF]).reshape(ROWS, PROBES, COLS)

        lane_group = lanes() // PROBES
        stays = halves[p, kept : kept + (PART if n == 0 else HALF)]
        own, other = halves[p, kept : kept + PART], halves[p, fresh : fresh + HALF]
        if n % 2 == 0:
            streamed = [(own, (0,)), (other, (0, 1))]
        else:
            streamed = [(halves[p, 0 : HALF + PART], (0, 1, 2))]
        blocks = []
        for left_rows, parts in streamed:
            product = lax.dot_general(left_rows, stays, (((1,), (1,)), ((), ())), preferred_element_type=F32)
            blocks += [product[q * PART : (q + 1) * PART] for q in parts]
        if n % 2:
            blocks = [blocks[2], blocks[0], blocks[1]]

        def equal_rows(block, c):
            chosen = block[0:PROBES, c : c + 128]
            for x in range(1, ROWS):
                chosen = jnp.where(lane_group == x, block[x * PROBES : (x + 1) * PROBES, c : c + 128], chosen)
            return chosen

        grams[n, 0] += equal_rows(blocks[0], 0)
        crossed = equal_rows(blocks[1], 0) + equal_rows(blocks[2], 0)
        if n:
            grams[n, 1] += equal_rows(blocks[0], PART)
            crossed = crossed + equal_rows(blocks[1], PART) + equal_rows(blocks[2], PART)
        grams[n, 2] += crossed

    sub = lax.broadcasted_iota(jnp.int32, (8, 128), 0)
    keep = sub == lanes() // PROBES

    def over_rows(total):
        for shift in (8, 16, 32, 64):
            total = total + pltpu.roll(total, shift, 1)
        return total

    def turned(total):
        return jnp.transpose(jnp.concatenate([total] * ROWS, 0))[0:PROBES]

    packed = jnp.zeros((8, 128), F32)
    for n in range(STEPS):
        pl.loop(0, PL)(functools.partial(step, n))
        even, odd = over_rows(grams[n, 0]), turned(over_rows(grams[n, 2]))
        if n:
            low = over_rows(grams[n, 1])
            even = even + low + turned(low)
        for m, total in ((2 * n, even), (2 * n + 1, odd)):
            row = jnp.sum(jnp.where(keep, total, 0.0), axis=0, keepdims=True)
            packed = jnp.where(sub == m, jnp.broadcast_to(row, (8, 128)), packed)
    flat[...] = packed

    first[gy] = packed
    copies = []
    for d in range(1, GYN):
        c = pltpu.make_async_remote_copy(
            flat, first.at[gy], sum_send.at[0, d], sum_recv.at[0, d],
            device_id=(gx, lax.rem(gy + d, GYN)), device_id_type=MESH,
        )
        c.start()
        copies.append(c)
    for n in range(STEPS):

        @pl.loop(0, PL)
        def _(p):
            for side in range(2):
                row_copy(n, p, side).wait_send()
                col_copy(n, p, side).wait_send()
    for d in range(1, GYN):
        pltpu.make_async_remote_copy(
            flat, first.at[lax.rem(gy + GYN - d, GYN)], sum_send.at[0, d], sum_recv.at[0, d],
            device_id=(gx, lax.rem(gy + d, GYN)), device_id_type=MESH,
        ).wait_recv()
    total = first[0]
    for d in range(1, GYN):
        total = total + first[d]
    second[gx] = total
    for d in range(1, GXN):
        c = pltpu.make_async_remote_copy(
            second.at[gx], second.at[gx], sum_send.at[1, d], sum_recv.at[1, d],
            device_id=(lax.rem(gx + d, GXN), gy), device_id_type=MESH,
        )
        c.start()
        copies.append(c)
    for c in copies[: GYN - 1]:
        c.wait_send()
    for d in range(1, GXN):
        source = lax.rem(gx + GXN - d, GXN)
        pltpu.make_async_remote_copy(
            second.at[source], second.at[source], sum_send.at[1, d], sum_recv.at[1, d],
            device_id=(lax.rem(gx + d, GXN), gy), device_id_type=MESH,
        ).wait_recv()
    total = second[0]
    for d in range(1, GXN):
        total = total + second[d]
    moments_out[...] = total

    for c in copies[GYN - 1 :]:
        c.wait_send()


def finish_kernel(vector, grams, table, green, out, table_here, out_sem, table_sem):
    device = lax.axis_index("gx") * GYN + lax.axis_index("gy")
    fetch = pltpu.make_async_copy(table.at[device], table_here, table_sem)
    fetch.start()
    copies = []
    for p in range(PL):
        for i in range(PROBES):
            c = pltpu.make_async_copy(vector.at[p, :, i, :], out.at[i, p], out_sem.at[p, i])
            c.start()
            copies.append(c)
    fetch.wait()
    scaled = grams[...] / SITES
    rows = [scaled[0:1], scaled[1:2]]
    for m in range(2, NMOM):
        rows.append(2.0 * scaled[m : m + 1] - rows[m % 2])
    moments = jnp.concatenate(rows + [jnp.zeros((128 - NMOM, 128), F32)], 0)
    weights = jnp.transpose(jnp.concatenate([table_here[...], jnp.zeros((128 - NMOM, 128), F32)], 0))
    result = jnp.dot(weights, moments, precision=lax.Precision.HIGHEST, preferred_element_type=F32)
    green[0] = result[0:EB, 0 : PROBES * PROBES]
    green[1] = result[EB : 2 * EB, 0 : PROBES * PROBES]
    for c in copies:
        c.wait()


def on_device(levels, probe_bits):
    anywhere = pl.BlockSpec(memory_space=pl.ANY)
    vmem = pl.BlockSpec(memory_space=pltpu.VMEM)
    dma = pltpu.SemaphoreType.DMA
    last, grams = pl.pallas_call(
        main_kernel,
        out_shape=(
            pltpu.VMEM((PL, ROWS, PROBES, COLS), F32),
            pltpu.VMEM((8, 128), F32),
        ),
        in_specs=[anywhere, anywhere],
        out_specs=(vmem, vmem),
        scratch_shapes=[
            pltpu.VMEM((PL + 2, ROWS + 2, PROBES, COLS), F32),
            pltpu.VMEM((PL + 2, ROWS + 2, PROBES, COLS), F32),
            pltpu.VMEM((PL + 2, ROWS + 2, PROBES, COLS), F32),
            pltpu.VMEM((PL + 2, ROWS + 2, PROBES, COLS), F32),
            pltpu.VMEM((PL, ROWS, PROBES, COLS), jnp.int32),
            pltpu.VMEM((PL, 2 * HALF, COLS), BF16),
            pltpu.VMEM((PL, ROWS, PROBES, COLS), F32),
            pltpu.VMEM((PL, ROWS, COLS), jnp.int32),
            pltpu.VMEM((BLOCK, BLOCK), BF16),
            pltpu.VMEM((BLOCK, BLOCK), BF16),
            pltpu.VMEM((STEPS, 2, PL, 8, 128), F32),
            pltpu.VMEM((STEPS, 2, PL, 8, 128), F32),
            pltpu.VMEM((STEPS, 3, 8, 128), F32),
            pltpu.VMEM((8, 128), F32),
            pltpu.VMEM((GYN, 8, 128), F32),
            pltpu.VMEM((GXN, 8, 128), F32),
            dma((STEPS, 2, PL)),
            dma((STEPS, 2, PL)),
            dma((STEPS, 2, PL)),
            dma((STEPS, 2, PL)),
            dma((PL, PROBES)),
            dma,
            dma((2, GYN)),
            dma((2, GYN)),
        ],
        compiler_params=pltpu.CompilerParams(
            collective_id=0, has_side_effects=True, vmem_limit_bytes=54 << 20
        ),
    )(levels, probe_bits)
    green, out = pl.pallas_call(
        finish_kernel,
        out_shape=(
            jax.ShapeDtypeStruct((2, EB, PROBES * PROBES), F32),
            jax.ShapeDtypeStruct((PROBES, PL, ROWS, COLS), F32),
        ),
        in_specs=[vmem, vmem, anywhere],
        out_specs=(vmem, anywhere),
        scratch_shapes=[
            pltpu.VMEM((NMOM, 2 * EB), F32),
            dma((PL, PROBES)),
            dma,
        ],
        compiler_params=pltpu.CompilerParams(vmem_limit_bytes=8 << 20),
    )(last, grams, jnp.asarray(energy_tables()))
    return green, out


def solution(mesh):
    return jax.shard_map(
        on_device,
        mesh=mesh,
        in_specs=(P(None, "gx", "gy"), P(None, None, "gx", "gy")),
        out_specs=(P(None, ("gx", "gy"), None), P(None, None, "gx", "gy")),
        check_vma=False,
    )
```

```python
import functools
import math

import jax
import jax.numpy as jnp
import numpy as np
from jax import lax
from jax.experimental import pallas as pl
from jax.experimental.pallas import tpu as pltpu
from jax.sharding import PartitionSpec as P

PROBES = 8
PL = 8
STEPS = 4
LEVELS = 8
NE = 8192
NMOM = 8
NX = 128
NY = 16384
SITES = 16777216
GXN = 8
GYN = 16
ROWS = NX // GXN
COLS = NY // GYN
TILES = COLS // 128
EB = NE // (GXN * GYN)
DEFER = 3
PART = ROWS * PROBES
HALF = 2 * PART
EACH = 4
BLOCK = 128 * EACH

disorder_width = 4.0
field_strength = 3.0
spectral_scale = 10.0
energy_edge = 0.9

MESH = pl.DeviceIdType.MESH
F32 = jnp.float32
BF16 = jnp.bfloat16


def energy_tables():
    theta = np.arccos(energy_edge * np.cos(math.pi * (np.arange(NE) + 0.5) / NE))
    total = NMOM + 1.0
    rows = []
    for m in range(NMOM):
        damp = (
            (NMOM - m + 1.0) * math.cos(math.pi * m / total)
            + math.sin(math.pi * m / total) / math.tan(math.pi / total)
        ) / total
        weight = damp if m == 0 else 2.0 * damp
        rows.append(
            np.stack(
                [
                    -weight * np.sin(m * theta) / np.sin(theta),
                    -weight * np.cos(m * theta) / np.sin(theta),
                ]
            )
        )
    table = np.stack(rows).reshape(NMOM, 2, GXN * GYN, EB)
    return np.ascontiguousarray(table.transpose(2, 0, 1, 3).reshape(GXN * GYN, NMOM, 2 * EB)).astype(np.float32)


def lanes():
    return lax.broadcasted_iota(jnp.int32, (8, 128), 1)


def split(pair):
    high = pair.astype(BF16)
    return high, (pair - high.astype(F32)).astype(BF16)


def main_kernel(
    levels, bits, last, moments_out,
    field0, field1, field2, field3, raw, halves, onsite, lev, mix, unmix,
    edge_out, edge_in, grams, flat, first, second,
    row_send, row_recv, col_send, col_recv, load_sem, lev_sem, sum_send, sum_recv,
):
    fields = (field0, field1, field2, field3)
    gx, gy = lax.axis_index("gx"), lax.axis_index("gy")
    up, down = (lax.rem(gx + GXN - 1, GXN), gy), (lax.rem(gx + 1, GXN), gy)
    left, right = (gx, lax.rem(gy + GYN - 1, GYN)), (gx, lax.rem(gy + 1, GYN))

    def row_copy(n, p, side):
        here, there = ((1, ROWS + 1), (ROWS, 0))[side]
        return pltpu.make_async_remote_copy(
            fields[n].at[p + 1, here], fields[n].at[p + 1, there],
            row_send.at[n, side, p], row_recv.at[n, side, p],
            device_id=(up, down)[side], device_id_type=MESH,
        )

    def col_copy(n, p, side):
        return pltpu.make_async_remote_copy(
            edge_out.at[n, side, p], edge_in.at[n, side, p],
            col_send.at[n, side, p], col_recv.at[n, side, p],
            device_id=(left, right)[side], device_id_type=MESH,
        )

    def send_rows(n, p):
        for side in range(2):
            row_copy(n, p, side).start()

    def send_edges(n, p, left_edge, right_edge):
        edge_out[n, 0, p] = left_edge
        edge_out[n, 1, p] = right_edge
        for side in range(2):
            col_copy(n, p, side).start()

    def load(p, i):
        return pltpu.make_async_copy(bits.at[i, p], raw.at[p, :, i, :], load_sem.at[p, i])

    barrier = pltpu.get_barrier_semaphore()
    for d in range(1, GXN):
        pl.semaphore_signal(barrier, inc=1, device_id=(lax.rem(gx + d, GXN), gy), device_id_type=MESH)
    for d in range(1, GYN):
        pl.semaphore_signal(barrier, inc=1, device_id=(gx, lax.rem(gy + d, GYN)), device_id_type=MESH)

    lev_copy = pltpu.make_async_copy(levels, lev, lev_sem)
    lev_copy.start()

    @pl.loop(0, PL)
    def _(p):
        for i in range(PROBES):
            load(p, i).start()

    source = lax.broadcasted_iota(jnp.int32, (BLOCK, BLOCK), 0)
    place = lax.broadcasted_iota(jnp.int32, (BLOCK, BLOCK), 1)
    mix[...] = jnp.where(source == lax.rem(place, 128) * EACH + place // 128, 1.0, 0.0).astype(BF16)
    unmix[...] = jnp.where(place == lax.rem(source, 128) * EACH + source // 128, 1.0, 0.0).astype(BF16)

    def moved(value, matrix):
        order = matrix[...]
        return jnp.concatenate(
            [
                lax.dot_general(
                    value[:, c : c + BLOCK], order, (((1,), (0,)), ((), ())), preferred_element_type=F32
                )
                for c in range(0, COLS, BLOCK)
            ],
            1,
        )

    def begin(p):
        for i in range(PROBES):
            load(p, i).wait()
        signs = (2 * raw[p] - 1).astype(F32).reshape(ROWS * PROBES, COLS)
        value = moved(signs.astype(BF16), mix)
        halves[p, 0 : ROWS * PROBES] = value.astype(BF16)
        left_edge, right_edge = jnp.zeros((8, 128), F32), jnp.zeros((8, 128), F32)
        lane = lanes()
        for x in range(ROWS):
            row = value[x * PROBES : (x + 1) * PROBES]
            field0[p + 1, x + 1] = row
            left_edge = jnp.where(lane == x, pltpu.roll(row[:, 0:128], x, 1), left_edge)
            right_edge = jnp.where(lane == x, pltpu.roll(row[:, COLS - 128 :], x + 1, 1), right_edge)
        return left_edge, right_edge

    for field in fields:
        for p in (0, PL + 1):

            @pl.loop(0, ROWS + 2)
            def _(x):
                field[p, x] = jnp.zeros((PROBES, COLS), F32)

    grams[...] = jnp.zeros_like(grams)

    lev_copy.wait()
    level = moved(lev[...].astype(F32).astype(BF16).reshape(PL * ROWS, COLS), mix)
    for x in range(ROWS):
        slope = field_strength * (((gx * ROWS + x).astype(F32) + 0.5) / NX - 0.5)
        for p in range(PL):
            at = p * ROWS + x
            value = disorder_width * (level[at : at + 1] / (LEVELS - 1) - 0.5) + slope
            onsite[p, x] = jnp.broadcast_to(value, (PROBES, COLS))

    pl.semaphore_wait(barrier, GXN + GYN - 2)

    @pl.loop(0, PL // 2)
    def _(q):
        send_edges(0, 2 * q, *begin(2 * q))
        send_rows(0, q)
        send_edges(0, 2 * q + 1, *begin(2 * q + 1))

    for p in range(PL // 2, PL - DEFER):
        send_rows(0, p)

    def step(n, p):
        field, base = fields[n], p + 1
        older = fields[n - 1] if n else None
        newer = fields[n + 1] if n + 1 < STEPS else None
        kept, fresh = (n % 2) * HALF, ((n + 1) % 2) * HALF
        for side in range(2):
            col_copy(n, p, side).wait_recv()
            row_copy(n, p, side).wait_recv()
        from_right, from_left = edge_in[n, 0, p], edge_in[n, 1, p]
        left_edge, right_edge = jnp.zeros((8, 128), F32), jnp.zeros((8, 128), F32)
        lane = lanes()
        is_first, is_last = lane == 0, lane == 127

        def tiles(x):
            return [field[base, x, :, t * 128 : (t + 1) * 128] for t in range(TILES)]

        above, now = tiles(0), tiles(1)
        pair = []
        for x in range(ROWS):
            below = tiles(x + 2)
            forth = [pltpu.roll(from_left, (128 - x) % 128, 1)]
            forth += [pltpu.roll(now[t], 1, 1) for t in range(EACH - 1, TILES, EACH)]
            back = [pltpu.roll(now[t], 127, 1) for t in range(0, TILES, EACH)]
            back += [pltpu.roll(from_right, 127 - x, 1)]
            around = []
            for t in range(TILES):
                block = t // EACH
                before = now[t - 1] if t % EACH else jnp.where(is_first, forth[block], forth[block + 1])
                beyond = now[t + 1] if (t + 1) % EACH else jnp.where(is_last, back[block + 1], back[block])
                around.append(beyond + before)
            made = []
            for t in range(TILES):
                cut = pl.ds(t * 128, 128)
                beside = (below[t] + above[t]) + around[t]
                beside = beside + (field[base + 1, x + 1, :, cut] + field[base - 1, x + 1, :, cut])
                hopped = onsite[p, x, :, cut] * now[t] - beside
                if n == 0:
                    value = hopped * (1.0 / spectral_scale)
                else:
                    value = hopped * (2.0 / spectral_scale) - older[base, x + 1, :, cut]
                if n + 1 < STEPS:
                    newer[base, x + 1, :, cut] = value
                made.append(value)
            if n + 1 < STEPS:
                left_edge = jnp.where(lane == x, pltpu.roll(made[0], x, 1), left_edge)
                right_edge = jnp.where(lane == x, pltpu.roll(made[TILES - 1], x + 1, 1), right_edge)
            pair.append(made)
            if len(pair) == 2:
                at = (x - 1) * PROBES
                for t in range(TILES):
                    cut = pl.ds(t * 128, 128)
                    high, low = split(jnp.concatenate([pair[0][t], pair[1][t]], 0))
                    halves[p, fresh + at : fresh + at + 16, cut] = high
                    halves[p, fresh + PART + at : fresh + PART + at + 16, cut] = low
                pair = []
            above, now = now, below

        if n + 1 < STEPS:
            send_edges(n + 1, p, left_edge, right_edge)
            if DEFER == 0:
                send_rows(n + 1, p)
            else:
                pl.when(p >= DEFER)(lambda: send_rows(n + 1, p - DEFER))
        if DEFER:
            pl.when(p < DEFER)(lambda: send_rows(n, p + PL - DEFER))

        if n + 1 == STEPS:
            both = moved(halves[p, fresh : fresh + HALF], unmix)
            last[p] = (both[0:PART] + both[PART:HALF]).reshape(ROWS, PROBES, COLS)

        lane_group = lanes() // PROBES
        stays = halves[p, kept : kept + (PART if n == 0 else HALF)]
        own, other = halves[p, kept : kept + PART], halves[p, fresh : fresh + HALF]
        if n % 2 == 0:
            streamed = [(own, (0,)), (other, (0, 1))]
        else:
            streamed = [(halves[p, 0 : HALF + PART], (0, 1, 2))]
        blocks = []
        for left_rows, parts in streamed:
            product = lax.dot_general(left_rows, stays, (((1,), (1,)), ((), ())), preferred_element_type=F32)
            blocks += [product[q * PART : (q + 1) * PART] for q in parts]
        if n % 2:
            blocks = [blocks[2], blocks[0], blocks[1]]

        def equal_rows(block, c):
            chosen = block[0:PROBES, c : c + 128]
            for x in range(1, ROWS):
                chosen = jnp.where(lane_group == x, block[x * PROBES : (x + 1) * PROBES, c : c + 128], chosen)
            return chosen

        grams[n, 0] += equal_rows(blocks[0], 0)
        crossed = equal_rows(blocks[1], 0) + equal_rows(blocks[2], 0)
        if n:
            grams[n, 1] += equal_rows(blocks[0], PART)
            crossed = crossed + equal_rows(blocks[1], PART) + equal_rows(blocks[2], PART)
        grams[n, 2] += crossed

    sub = lax.broadcasted_iota(jnp.int32, (8, 128), 0)
    keep = sub == lanes() // PROBES

    def over_rows(total):
        for shift in (8, 16, 32, 64):
            total = total + pltpu.roll(total, shift, 1)
        return total

    def turned(total):
        return jnp.transpose(jnp.concatenate([total] * ROWS, 0))[0:PROBES]

    packed = jnp.zeros((8, 128), F32)
    for n in range(STEPS):
        pl.loop(0, PL)(functools.partial(step, n))
        even, odd = over_rows(grams[n, 0]), turned(over_rows(grams[n, 2]))
        if n:
            low = over_rows(grams[n, 1])
            even = even + low + turned(low)
        for m, total in ((2 * n, even), (2 * n + 1, odd)):
            row = jnp.sum(jnp.where(keep, total, 0.0), axis=0, keepdims=True)
            packed = jnp.where(sub == m, jnp.broadcast_to(row, (8, 128)), packed)
    flat[...] = packed

    first[gy] = packed
    copies = []
    for d in range(1, GYN):
        c = pltpu.make_async_remote_copy(
            flat, first.at[gy], sum_send.at[0, d], sum_recv.at[0, d],
            device_id=(gx, lax.rem(gy + d, GYN)), device_id_type=MESH,
        )
        c.start()
        copies.append(c)
    for n in range(STEPS):

        @pl.loop(0, PL)
        def _(p):
            for side in range(2):
                row_copy(n, p, side).wait_send()
                col_copy(n, p, side).wait_send()
    for d in range(1, GYN):
        pltpu.make_async_remote_copy(
            flat, first.at[lax.rem(gy + GYN - d, GYN)], sum_send.at[0, d], sum_recv.at[0, d],
            device_id=(gx, lax.rem(gy + d, GYN)), device_id_type=MESH,
        ).wait_recv()
    total = first[0]
    for d in range(1, GYN):
        total = total + first[d]
    second[gx] = total
    for d in range(1, GXN):
        c = pltpu.make_async_remote_copy(
            second.at[gx], second.at[gx], sum_send.at[1, d], sum_recv.at[1, d],
            device_id=(lax.rem(gx + d, GXN), gy), device_id_type=MESH,
        )
        c.start()
        copies.append(c)
    for c in copies[: GYN - 1]:
        c.wait_send()
    for d in range(1, GXN):
        source = lax.rem(gx + GXN - d, GXN)
        pltpu.make_async_remote_copy(
            second.at[source], second.at[source], sum_send.at[1, d], sum_recv.at[1, d],
            device_id=(lax.rem(gx + d, GXN), gy), device_id_type=MESH,
        ).wait_recv()
    total = second[0]
    for d in range(1, GXN):
        total = total + second[d]
    moments_out[...] = total

    for c in copies[GYN - 1 :]:
        c.wait_send()


def finish_kernel(vector, grams, table, green, out, table_here, out_sem, table_sem):
    device = lax.axis_index("gx") * GYN + lax.axis_index("gy")
    fetch = pltpu.make_async_copy(table.at[device], table_here, table_sem)
    fetch.start()
    copies = []
    for p in range(PL):
        for i in range(PROBES):
            c = pltpu.make_async_copy(vector.at[p, :, i, :], out.at[i, p], out_sem.at[p, i])
            c.start()
            copies.append(c)
    fetch.wait()
    scaled = grams[...] / SITES
    rows = [scaled[0:1], scaled[1:2]]
    for m in range(2, NMOM):
        rows.append(2.0 * scaled[m : m + 1] - rows[m % 2])
    moments = jnp.concatenate(rows + [jnp.zeros((128 - NMOM, 128), F32)], 0)
    weights = jnp.transpose(jnp.concatenate([table_here[...], jnp.zeros((128 - NMOM, 128), F32)], 0))
    result = jnp.dot(weights, moments, precision=lax.Precision.HIGHEST, preferred_element_type=F32)
    green[0] = result[0:EB, 0 : PROBES * PROBES]
    green[1] = result[EB : 2 * EB, 0 : PROBES * PROBES]
    for c in copies:
        c.wait()


def on_device(levels, probe_bits):
    anywhere = pl.BlockSpec(memory_space=pl.ANY)
    vmem = pl.BlockSpec(memory_space=pltpu.VMEM)
    dma = pltpu.SemaphoreType.DMA
    last, grams = pl.pallas_call(
        main_kernel,
        out_shape=(
            pltpu.VMEM((PL, ROWS, PROBES, COLS), F32),
            pltpu.VMEM((8, 128), F32),
        ),
        in_specs=[anywhere, anywhere],
        out_specs=(vmem, vmem),
        scratch_shapes=[
            pltpu.VMEM((PL + 2, ROWS + 2, PROBES, COLS), F32),
            pltpu.VMEM((PL + 2, ROWS + 2, PROBES, COLS), F32),
            pltpu.VMEM((PL + 2, ROWS + 2, PROBES, COLS), F32),
            pltpu.VMEM((PL + 2, ROWS + 2, PROBES, COLS), F32),
            pltpu.VMEM((PL, ROWS, PROBES, COLS), jnp.int32),
            pltpu.VMEM((PL, 2 * HALF, COLS), BF16),
            pltpu.VMEM((PL, ROWS, PROBES, COLS), F32),
            pltpu.VMEM((PL, ROWS, COLS), jnp.int32),
            pltpu.VMEM((BLOCK, BLOCK), BF16),
            pltpu.VMEM((BLOCK, BLOCK), BF16),
            pltpu.VMEM((STEPS, 2, PL, 8, 128), F32),
            pltpu.VMEM((STEPS, 2, PL, 8, 128), F32),
            pltpu.VMEM((STEPS, 3, 8, 128), F32),
            pltpu.VMEM((8, 128), F32),
            pltpu.VMEM((GYN, 8, 128), F32),
            pltpu.VMEM((GXN, 8, 128), F32),
            dma((STEPS, 2, PL)),
            dma((STEPS, 2, PL)),
            dma((STEPS, 2, PL)),
            dma((STEPS, 2, PL)),
            dma((PL, PROBES)),
            dma,
            dma((2, GYN)),
            dma((2, GYN)),
        ],
        compiler_params=pltpu.CompilerParams(
            collective_id=0, has_side_effects=True, vmem_limit_bytes=54 << 20
        ),
    )(levels, probe_bits)
    green, out = pl.pallas_call(
        finish_kernel,
        out_shape=(
            jax.ShapeDtypeStruct((2, EB, PROBES * PROBES), F32),
            jax.ShapeDtypeStruct((PROBES, PL, ROWS, COLS), F32),
        ),
        in_specs=[vmem, vmem, anywhere],
        out_specs=(vmem, anywhere),
        scratch_shapes=[
            pltpu.VMEM((NMOM, 2 * EB), F32),
            dma((PL, PROBES)),
            dma,
        ],
        compiler_params=pltpu.CompilerParams(vmem_limit_bytes=8 << 20),
    )(last, grams, jnp.asarray(energy_tables()))
    return green, out


def solution(mesh):
    return jax.shard_map(
        on_device,
        mesh=mesh,
        in_specs=(P(None, "gx", "gy"), P(None, None, "gx", "gy")),
        out_specs=(P(None, ("gx", "gy"), None), P(None, None, "gx", "gy")),
        check_vma=False,
    )
```
